256 devices in a mesh: dp: 16 (over z, core), expert: 4 (over y), blk: 4 (over x).
Axes of the slice: x: 4, y: 4, z: 8, core: 2. Of those that a mesh axis runs over, the one named last changes fastest.
Arguments:
- tokens: bfloat16 [2048, 6144], P('dp', 'blk'), may hold values from -6 to 6
- expert_ids: int32 [2048, 2], P('dp'), may hold values from 0 to 7, all different within a row; in each aligned block of 128 rows (0 to 127, 128 to 255, ...) at most 48 rows name the same one
- route_weights: float32 [2048, 2], P('dp'), may hold values from 0.1 to 1
- gate_weight: bfloat16 [8, 6144, 8192], P('expert', 'blk', 'dp'), may hold values from -0.078125 to 0.078125
- up_weight: bfloat16 [8, 6144, 8192], P('expert', 'blk', 'dp'), may hold values from -0.078125 to 0.078125
- down_weight: bfloat16 [8, 8192, 6144], P('expert', 'dp', 'blk'), may hold values from -0.0625 to 0.0625
Outputs:
- mixed: bfloat16 [2048, 6144], P('dp', 'blk')
The draws below stay inside these ranges and needn't reach their ends.
Inputs may be any that keep to these rules, and one draw needn't show every extreme that they name: `expert_ids`: each row names 2 different experts. Among the 128 rows of one data shard no expert is named more than 48 times, and in every draw some expert is named exactly 48 times in some shard.
All inputs are finite; a program needn't handle non-finite values.
Results may differ from the reference program's by a relative error of at most 0.0051.
Values may be sent and summed in bfloat16 or wider, within the bound.
A program may use at most 64 MiB of HBM per device.

```python
import math
import jax
import jax.numpy as jnp
import numpy as np
from jax import lax

D = 6144
EXPERTS = 8
FFW = 8192
TOP = 2
TOK_DEV = 128
CAP = 48
TOKENS = 2048
N_DP = 16


def block_levels(key, dims, split, low, top_value):
    level, own = 1.0, jax.random.fold_in(key, 6)
    for axis_at, blocks in split:
        steps = jnp.exp(jax.random.uniform(jax.random.fold_in(own, axis_at), (blocks,), jnp.float32, low / len(split), top_value / len(split)))
        level = level * jnp.repeat(steps, dims[axis_at] // blocks).reshape([-1 if axis == axis_at else 1 for axis in range(len(dims))])
    return level


def routed_block(rng, own, number, rows, amount, top, limit, skew):
    order = jax.random.permutation(rng, amount)
    heavy_load, ordinary = load_shares(amount, rows * top, limit, skew, True), load_shares(amount, rows * top, limit, skew, False)
    places = jnp.arange(amount)

    def named(tallies, turn):
        used = int((tallies > 0).sum())
        fixed = max(1, used // 4)
        passed = fixed + (places - fixed + turn * (used - fixed)) % max(1, amount - fixed)
        return jnp.zeros((amount,), jnp.int32).at[order[jnp.where(places < fixed, places, passed)]].set(jnp.asarray(tallies, jnp.int32))

    tallies = jnp.where(number % 4 == 0, named(heavy_load, number // 4), named(ordinary, number - number // 4 - 1))
    mixed = jax.random.permutation(jax.random.fold_in(own, 3), amount)
    source_of, sink = mixed[0:amount // 2 * 2:2], mixed[1:amount // 2 * 2:2]
    room = jnp.minimum(tallies[source_of] - 1, limit - tallies[sink]) // 2
    room = jnp.where((source_of == order[0]) | (sink == order[0]) | (tallies[sink] == 0), 0, jnp.maximum(room, 0))
    passed = jax.random.randint(jax.random.fold_in(own, 4), (amount // 2,), 0, 1 << 20) % (room + 1)
    tallies = tallies.at[source_of].add(-passed).at[sink].add(passed)
    labels = jnp.searchsorted(jnp.cumsum(tallies), jnp.arange(rows * top), side="right").astype(jnp.int32)
    grid = labels.reshape(top, rows).T
    grid = grid[jax.random.permutation(jax.random.fold_in(own, 1), rows)]
    turn = jax.random.randint(jax.random.fold_in(own, 2), (rows, 1), 0, top)
    return jnp.take_along_axis(grid, (jnp.arange(top)[None, :] + turn) % top, axis=1)


def load_shares(amount, total, bound, lean, full):
    loads = [(1 << 20) // math.isqrt(standing ** lean) + 1 for standing in range(1, amount + 1)]
    largest = bound if full else min(bound, max(-(-total // amount), total * loads[0] // sum(loads)))
    least = 1 if total - largest >= amount - 1 else 0
    holding, rest = [largest] + [least] * (amount - 1), total - largest - least * (amount - 1)
    while rest > 0:
        free = [i for i in range(1, amount) if holding[i] < largest] or [i for i in range(1, amount) if holding[i] < bound]
        whole, left = sum([loads[i] for i in free]), rest
        for i in free:
            extra = min(bound - holding[i], max(1, left * loads[i] // whole), rest)
            holding[i] = holding[i] + extra
            rest = rest - extra
    return np.array(holding)


def normal_values(stream_key, extent, spread, most, cuts=(), held_as=jnp.bfloat16):
    result = jax.random.normal(stream_key, extent, jnp.float32) * spread
    if len(cuts) > 0:
        result = block_levels(stream_key, extent, cuts, -0.22, 0.18) * result
    return jnp.clip(result, min=-most, max=most).astype(held_as)


def setup_inputs(seed: int = 0) -> dict:
    key_of = jax.random.split(jax.random.key(seed), 7)
    tokens = normal_values(key_of[0], (TOKENS, D), 1.0, 6.0, ((0, 16), (1, 4)))
    expert_ids_keys = jax.random.split(jax.random.fold_in(key_of[1], 1), TOKENS // TOK_DEV)
    expert_ids_turns = jax.random.permutation(jax.random.fold_in(key_of[1], 3), TOKENS // TOK_DEV)
    expert_ids = jax.vmap(lambda own, number: routed_block(jax.random.fold_in(key_of[1], 2), own, number, TOK_DEV, EXPERTS, TOP, CAP, 2))(expert_ids_keys, expert_ids_turns).reshape((TOKENS, TOP))
    route_weights = jnp.clip(0.1 + 0.9 * jax.random.uniform(key_of[2], (TOKENS, TOP), jnp.float32) ** block_levels(key_of[2], (TOKENS, TOP), ((0, 16),), -0.2, 0.2), 0.1, 1.0)
    gate_weight = normal_values(key_of[3], (EXPERTS, D, FFW), D ** -0.5, 0.078125, ((0, 4), (1, 4), (2, 16)))
    up_weight = normal_values(key_of[4], (EXPERTS, D, FFW), D ** -0.5, 0.078125, ((0, 4), (1, 4), (2, 16)))
    down_weight = normal_values(key_of[5], (EXPERTS, FFW, D), FFW ** -0.5, 0.0625, ((0, 4), (1, 16), (2, 4)))
    return {"tokens": tokens, "expert_ids": expert_ids, "route_weights": route_weights, "gate_weight": gate_weight, "up_weight": up_weight, "down_weight": down_weight}


def reference(tokens, expert_ids, route_weights, gate_weight, up_weight, down_weight):
    shards = N_DP
    flat_ids = expert_ids.reshape(shards, TOK_DEV * TOP)
    one_hot = (flat_ids[:, :, None] == jnp.arange(EXPERTS, dtype=jnp.int32)[None, None, :]).astype(jnp.int32)
    before = jnp.cumsum(one_hot, axis=1) - one_hot
    position = jnp.sum(before * one_hot, axis=2)
    weights = route_weights.reshape(shards, TOK_DEV, TOP)
    token_blocks = tokens.reshape(shards, TOK_DEV, D).astype(jnp.float32)
    slot_ids = jnp.arange(CAP, dtype=jnp.int32)

    def one_expert(accumulated, expert):
        slot_hit = (flat_ids == expert)[:, :, None] & (position[:, :, None] == slot_ids[None, None, :])
        slot_hit = slot_hit.reshape(shards, TOK_DEV, TOP, CAP)
        dispatch = jnp.any(slot_hit, axis=2).astype(jnp.float32)
        combine = jnp.sum(slot_hit.astype(jnp.float32) * weights[:, :, :, None], axis=2)
        picked = jnp.einsum("stc,std->scd", dispatch, token_blocks, precision=lax.Precision.HIGHEST).astype(jnp.bfloat16)
        picked = picked.reshape(shards * CAP, D)
        gate = jnp.dot(picked, lax.dynamic_index_in_dim(gate_weight, expert, 0, keepdims=False), preferred_element_type=jnp.float32)
        up = jnp.dot(picked, lax.dynamic_index_in_dim(up_weight, expert, 0, keepdims=False), preferred_element_type=jnp.float32)
        hidden = (jax.nn.silu(gate) * up).astype(jnp.bfloat16)
        expert_out = jnp.dot(hidden, lax.dynamic_index_in_dim(down_weight, expert, 0, keepdims=False), preferred_element_type=jnp.float32)
        expert_out = expert_out.reshape(shards, CAP, D)
        accumulated = accumulated + jnp.einsum("stc,scd->std", combine, expert_out, precision=lax.Precision.HIGHEST)
        return accumulated, None

    start_sum = jnp.zeros((shards, TOK_DEV, D), jnp.float32)
    summed, unused = lax.scan(one_expert, start_sum, jnp.arange(EXPERTS, dtype=jnp.int32))
    return summed.reshape(TOKENS, D).astype(jnp.bfloat16)
```

```python
import functools

import jax
import jax.numpy as jnp
from jax import lax
from jax.experimental import pallas as pl
from jax.experimental.pallas import tpu as pltpu
from jax.sharding import PartitionSpec as P

MESH = pl.DeviceIdType.MESH
CAP = 48
NZ, NY, NX = 8, 4, 4
UNITS = 16
SUB = 2
L2, L3, L5, L6 = 2, 4, 6, 8
LC0, LC1 = 12, 16
SLOTS = LC1 + 8

F32, BF16 = jnp.float32, jnp.bfloat16


def dot(a, b, precision=None):
    return lax.dot_general(
        a, b, (((1,), (0,)), ((), ())), precision=precision, preferred_element_type=F32
    )


def slot_hits(ids, expert_of, slot_of):
    rows, lanes = ids.shape[0], slot_of.shape[1]
    first = jnp.broadcast_to(ids[:, 0:1], (rows, lanes)) == expert_of
    second = jnp.broadcast_to(ids[:, 1:2], (rows, lanes)) == expert_of
    named = jnp.where(first | second, 1.0, 0.0)
    earlier = lax.broadcasted_iota(jnp.int32, (rows, rows), 1) < lax.broadcasted_iota(
        jnp.int32, (rows, rows), 0
    )
    position = dot(jnp.where(earlier, 1.0, 0.0).astype(BF16), named.astype(BF16))
    here = position == slot_of.astype(F32)
    return first, second, jnp.where(here, named, 0.0)


def kernel(
    tok_ref, ids_ref, rw_ref, wg_hbm, wu_hbm, wd_hbm, out_ref,
    wg, wu, wd, xs, part, s_out, r_opp, r_sum, hid, own, pair_out, pair_in,
    c_out, c_in, eo0, eo1, comb,
    w_sem, a_ss, a_rs, p_ss, p_rs, x_ss, x_rs, q_ss, q_rs, c_ss, c_rs, y_ss, y_rs,
):
    dp, y, x = lax.axis_index("dp"), lax.axis_index("expert"), lax.axis_index("blk")
    z, c = dp // 2, dp % 2
    width = tok_ref.shape[1]
    sub_w = width // SUB
    partner = (z * 2 + (1 - c), y, x)
    right, left = (dp, y, (x + 1) % NX), (dp, y, (x + NX - 1) % NX)
    q_right, q_left, q_far = (x + 1) % NX, (x + NX - 1) % NX, (x + 2) % NX

    def zdev(step):
        return (((z + step + NZ) % NZ) * 2 + c, y, x)

    def ydev(step):
        return (dp, (y + step) % NY, x)

    def zchip(i):
        k = (i + 1) // 2
        return (z + k * (1 - 2 * (i % 2)) + NZ) % NZ

    def remote(src, dst, ss, rs, dev):
        return pltpu.make_async_remote_copy(
            src_ref=src, dst_ref=dst, send_sem=ss, recv_sem=rs, device_id=dev, device_id_type=MESH
        )

    weights = [
        pltpu.make_async_copy(h.at[e], v.at[e], w_sem.at[n, e])
        for e in range(2)
        for n, (h, v) in enumerate(((wg_hbm, wg), (wu_hbm, wu), (wd_hbm, wd)))
    ]
    for w in weights:
        w.start()

    barrier = pltpu.get_barrier_semaphore()
    peers = [partner, zdev(1), zdev(-1), right, left, ydev(1), ydev(2), ydev(3)]
    for d in peers:
        pl.semaphore_signal(barrier, inc=1, device_id=d, device_id_type=MESH)

    ids = ids_ref[...]
    lane = lax.broadcasted_iota(jnp.int32, (128, 128), 1)
    for e in range(2):
        _, _, hit = slot_hits(ids, 2 * y + e, lane)
        rows = lax.dot_general(
            hit.astype(BF16), tok_ref[...], (((0,), (0,)), ((), ())), preferred_element_type=F32
        )[:CAP].astype(BF16)
        for s in range(SUB):
            xs[e, s, dp] = rows[:, s * sub_w : (s + 1) * sub_w]
    pl.semaphore_wait(barrier, len(peers))

    def a_copy(e, s, chip, i, step):
        at = xs.at[e, s, 2 * chip + c]
        return remote(at, at, a_ss.at[e, i, s], a_rs.at[e, i, s], zdev(step))

    def p_copy(e, s, chip, i, core):
        at = xs.at[e, s, 2 * chip + core]
        return remote(at, at, p_ss.at[e, i, s], p_rs.at[e, i, s], partner)

    def send_own(e):
        for s in range(SUB):
            a_copy(e, s, z, 1, 1).start()
            a_copy(e, s, z, 2, -1).start()
            p_copy(e, s, z, 0, c).start()

    def pass_on(t):
        e, m = t // 4, t % 4
        for s in range(SUB):
            i = 2 * m + 1
            chip = zchip(i)
            a_copy(e, s, chip, i, 1).wait_recv()

            @pl.when((m < 2) | ((m == 2) & (e == 0)))
            def _():
                a_copy(e, s, chip, i + 2, 1).start()

            p_copy(e, s, chip, i, c).start()

            @pl.when(m < 3)
            def _():
                i = 2 * m + 2
                chip = zchip(i)
                a_copy(e, s, chip, i, -1).wait_recv()

                @pl.when((m < 2) | (e == 1))
                def _():
                    a_copy(e, s, chip, i + 2 - i // 6, -1).start()

                p_copy(e, s, chip, i, c).start()

    def unit(u):
        e, j = u // 8, u % 8
        i0 = j + (j // 4) * (11 - 2 * j)
        i = i0 + e * (7 - j - i0)
        return e, i, e * 8 + i

    def x_copy(v, n):
        src, dst, dev = (
            lambda: (s_out.at[v, q_far, 0], r_opp.at[v, 0], right),
            lambda: (s_out.at[v, q_far, 1], r_opp.at[v, 1], left),
            lambda: (s_out.at[v, q_right, 1], r_sum.at[v, 0, 1], right),
            lambda: (s_out.at[v, q_left, 0], r_sum.at[v, 1, 0], left),
            lambda: (s_out.at[v, q_right, 0], r_sum.at[v, 0, 0], right),
            lambda: (s_out.at[v, q_left, 1], r_sum.at[v, 1, 1], left),
            lambda: (hid.at[v, x], hid.at[v, x], right),
            lambda: (hid.at[v, x], hid.at[v, x], left),
            lambda: (hid.at[v, q_left, 0], hid.at[v, q_left, 0], right),
            lambda: (hid.at[v, q_right, 1], hid.at[v, q_right, 1], left),
        )[n]()
        return remote(src, dst, x_ss.at[v, n], x_rs.at[v, n], dev)

    def x_landed(v, n):
        at = (
            r_opp.at[v, 0],
            r_opp.at[v, 1],
            r_sum.at[v, 0, 1],
            r_sum.at[v, 1, 0],
            r_sum.at[v, 0, 0],
            r_sum.at[v, 1, 1],
            hid.at[v, q_left],
            hid.at[v, q_right],
            hid.at[v, q_far, 0],
            hid.at[v, q_far, 1],
        )[n]
        remote(at, at, x_ss.at[v, n], x_rs.at[v, n], right if n % 2 else left).wait_recv()

    def first(u):
        e, i, v = unit(u)
        chip = zchip(i)

        @pl.when(u % 8 == 0)
        def _():
            pltpu.make_async_copy(wg_hbm.at[e], wg.at[e], w_sem.at[0, e]).wait()
            pltpu.make_async_copy(wu_hbm.at[e], wu.at[e], w_sem.at[1, e]).wait()

        for s in range(SUB):
            p_copy(e, s, chip, i, 1 - c).wait_recv()
        rows = [xs[e, s, pl.ds(2 * chip, 2)].reshape(2 * CAP, sub_w) for s in range(SUB)]
        for g, w in enumerate((wg, wu)):
            total = sum(dot(rows[s], w[e, s * sub_w : (s + 1) * sub_w]) for s in range(SUB))
            for q in range(NX):
                block = total[:, q * 128 : (q + 1) * 128]
                for h in range(2):
                    half = block[h * CAP : (h + 1) * CAP]
                    part[v, q, h, g] = half
                    s_out[v, q, h, g] = half.astype(BF16)
        for n in range(4):
            x_copy(v, n).start()

    def second(u):
        _, _, v = unit(u)
        x_landed(v, 0)
        s_out[v, q_right, 0] = (part[v, q_right, 0] + r_opp[v, 0].astype(F32)).astype(BF16)
        x_copy(v, 4).start()
        x_landed(v, 1)
        s_out[v, q_left, 1] = (part[v, q_left, 1] + r_opp[v, 1].astype(F32)).astype(BF16)
        x_copy(v, 5).start()

    def third(u):
        _, _, v = unit(u)
        for n in range(2, 6):
            x_landed(v, n)
        for h in range(2):
            both = part[v, x, h] + r_sum[v, 0, h].astype(F32) + r_sum[v, 1, h].astype(F32)
            gate, up = both[0], both[1]
            hid[v, x, h] = (gate / (1.0 + jnp.exp(-gate)) * up).astype(BF16)
        x_copy(v, 6).start()
        x_copy(v, 7).start()

    def fifth(u):
        _, _, v = unit(u)
        x_landed(v, 6)
        x_copy(v, 8).start()
        x_landed(v, 7)
        x_copy(v, 9).start()

    def q_copy(v):
        return remote(pair_out.at[v], pair_in.at[v], q_ss.at[v], q_rs.at[v], partner)

    def sixth(u):
        e, i, v = unit(u)

        @pl.when(u % 8 == 0)
        def _():
            pltpu.make_async_copy(wd_hbm.at[e], wd.at[e], w_sem.at[2, e]).wait()

        x_landed(v, 8)
        x_landed(v, 9)
        rows = jnp.concatenate(
            [
                jnp.concatenate([hid[v, q, h] for q in range(NX)], axis=1)
                for h in (c, 1 - c)
            ],
            axis=0,
        )
        for n in range(width // 512):
            cols = slice(n * 512, (n + 1) * 512)
            block = dot(rows, wd[e, :, cols])
            own[v, :, cols] = block[:CAP]
            pair_out[v, :, cols] = block[CAP:]
        q_copy(v).start()
        for n in range(10):
            x_copy(v, n).wait_send()

    def c_copy(e, i, step):
        v = e * 8 + i
        return remote(c_out.at[v], c_in.at[v], c_ss.at[v], c_rs.at[v], zdev(step))

    def y_copy(e, o):
        buf = (eo0, eo1)[e]
        return remote(buf.at[y], buf.at[y], y_ss.at[e, o], y_rs.at[e, o], ydev(o))

    def y_landed(e, o):
        at = (eo0, eo1)[e].at[(y + NY - o) % NY]
        remote(at, at, y_ss.at[e, o], y_rs.at[e, o], ydev(o)).wait_recv()

    def reduce_z(e, j):
        i = 7 - j
        v = e * 8 + i
        q_copy(v).wait_recv()

        def from_up(slot):
            c_copy(e, slot, 1).wait_recv()
            return c_in[e * 8 + slot].astype(F32)

        def send():
            step = 1 - 2 * (i % 2)
            c_copy(e, i, step).start()

        no_up = (j == 0) | (j == (2 if e else 1))

        @pl.when(no_up)
        def _():
            c_out[v] = (own[v] + pair_in[v]).astype(BF16)

        @pl.when((j < 7) & jnp.logical_not(no_up))
        def _():
            c_out[v] = (own[v] + pair_in[v] + from_up(i + 2 - i // 6)).astype(BF16)

        if e == 0:

            @pl.when(j < 7)
            def _():
                send()
        else:

            @pl.when(j == 0)
            def _():
                c_copy(e, 7, 1).start()

            @pl.when((j > 0) & (j < 7))
            def _():
                send()

        @pl.when(j == 7)
        def _():
            total = own[v] + pair_in[v] + from_up(1) + from_up(2)
            if e == 0:
                eo0[y] = total
            else:
                eo1[y] = total.astype(BF16)
            for o in range(1, NY):
                y_copy(e, o).start()

    send_own(0)

    lanes = NY * CAP
    slot = lax.broadcasted_iota(jnp.int32, (128, lanes), 1)
    for e in range(2):
        expert_of = 2 * (slot // CAP) + e
        one, two, hit = slot_hits(ids, expert_of, slot % CAP)
        weight = jnp.where(one, rw_ref[:, 0:1], 0.0) + jnp.where(two, rw_ref[:, 1:2], 0.0)
        comb[e] = weight * hit

    def body(t, carry):
        def within(lag, count, f):
            @pl.when((t >= lag) & (t < lag + count))
            def _():
                f(t - lag)

        within(0, UNITS, first)

        @pl.when(t == 1)
        def _():
            send_own(1)

        within(0, 8, pass_on)
        within(L6, UNITS, sixth)
        within(L5, UNITS, fifth)
        within(L3, UNITS, third)
        within(L2, UNITS, second)
        within(LC0, 8, functools.partial(reduce_z, 0))
        within(LC1, 8, functools.partial(reduce_z, 1))
        return carry

    lax.fori_loop(0, SLOTS, body, 0)

    highest = lax.Precision.HIGHEST
    for o in range(1, NY):
        y_landed(0, o)
    total = dot(comb[0], eo0[...].reshape(lanes, width), highest)

    for e in range(2):

        def sent(i, carry):
            v = e * 8 + i
            q_copy(v).wait_send()
            for s in range(SUB):
                p_copy(e, s, z, i, c).wait_send()

            @pl.when(i > 0)
            def _():
                c_copy(e, i, 1).wait_send()
                for s in range(SUB):
                    a_copy(e, s, z, i, 1).wait_send()

            return carry

        lax.fori_loop(0, 8, sent, 0)
        for o in range(1, NY):
            y_copy(e, o).wait_send()

    for o in range(1, NY):
        y_landed(1, o)
    late = eo1[...].reshape(lanes, width).astype(F32)
    out_ref[...] = (total + dot(comb[1], late, highest)).astype(BF16)


def local(tokens, expert_ids, route_weights, gate_weight, up_weight, down_weight):
    rows, width = tokens.shape
    hidden = gate_weight.shape[2]
    quarter = hidden // NX
    vmem = pl.BlockSpec(memory_space=pltpu.VMEM)
    hbm = pl.BlockSpec(memory_space=pl.ANY)
    dma = pltpu.SemaphoreType.DMA
    return pl.pallas_call(
        kernel,
        out_shape=jax.ShapeDtypeStruct((rows, width), BF16),
        in_specs=[vmem, vmem, vmem, hbm, hbm, hbm],
        out_specs=vmem,
        scratch_shapes=[
            pltpu.VMEM(gate_weight.shape, BF16),
            pltpu.VMEM(up_weight.shape, BF16),
            pltpu.VMEM(down_weight.shape, BF16),
            pltpu.VMEM((2, SUB, 2 * NZ, CAP, width // SUB), BF16),
            pltpu.VMEM((UNITS, NX, 2, 2, CAP, quarter), F32),
            pltpu.VMEM((UNITS, NX, 2, 2, CAP, quarter), BF16),
            pltpu.VMEM((UNITS, 2, 2, CAP, quarter), BF16),
            pltpu.VMEM((UNITS, 2, 2, 2, CAP, quarter), BF16),
            pltpu.VMEM((UNITS, NX, 2, CAP, quarter), BF16),
            pltpu.VMEM((UNITS, CAP, width), F32),
            pltpu.VMEM((UNITS, CAP, width), F32),
            pltpu.VMEM((UNITS, CAP, width), F32),
            pltpu.VMEM((UNITS, CAP, width), BF16),
            pltpu.VMEM((UNITS, CAP, width), BF16),
            pltpu.VMEM((NY, CAP, width), F32),
            pltpu.VMEM((NY, CAP, width), BF16),
            pltpu.VMEM((2, rows, NY * CAP), F32),
            dma((3, 2)),
            dma((2, 8, SUB)),
            dma((2, 8, SUB)),
            dma((2, 8, SUB)),
            dma((2, 8, SUB)),
            dma((UNITS, 10)),
            dma((UNITS, 10)),
            dma((UNITS,)),
            dma((UNITS,)),
            dma((UNITS,)),
            dma((UNITS,)),
            dma((2, NY)),
            dma((2, NY)),
        ],
        compiler_params=pltpu.CompilerParams(
            collective_id=0, has_side_effects=True, vmem_limit_bytes=60 * 2**20
        ),
    )(tokens, expert_ids, route_weights, gate_weight, up_weight, down_weight)


def solution(mesh):
    placed = (
        P("dp", "blk"),
        P("dp", None),
        P("dp", None),
        P("expert", "blk", "dp"),
        P("expert", "blk", "dp"),
        P("expert", "dp", "blk"),
    )
    return jax.shard_map(
        local, mesh=mesh, in_specs=placed, out_specs=P("dp", "blk"), check_vma=False
    )
```

```python
import functools

import jax
import jax.numpy as jnp
from jax import lax
from jax.experimental import pallas as pl
from jax.experimental.pallas import tpu as pltpu
from jax.sharding import PartitionSpec as P

MESH = pl.DeviceIdType.MESH
CAP = 48
NZ, NY, NX = 8, 4, 4
UNITS = 16
SUB = 2
CUT = 3

STEPS = [
    128, 97, 4, 8, 5, 9, 96, 192, 160, 136, 16, 12, 256, 132, 17, 41,
    13, 144, 224, 140, 40, 20, 24, 168, 200, 21, 196, 25, 36, 148, 49, 152,
    204, 37, 28, 208, 29, 48, 156, 57, 164, 216, 176, 56, 220, 212, 61, 44,
    272, 280, 60, 45, 284, 188, 276, 268, 260, 172, 408, 184, 412, 52, 400, 472,
    53, 476, 477, 384, 404, 473, 252, 478, 264, 474, 180, 468, 396, 240, 469, 464,
    316, 470, 465, 466, 248, 460, 288, 392, 244, 304, 388, 461, 236, 444, 456, 452,
    312, 462, 508, 308, 232, 509, 453, 510, 228, 432, 457, 448, 458, 300, 416, 454,
    440, 436, 296, 504, 292, 500, 505, 449, 501, 428, 502, 496, 506, 450, 492, 424,
    420, 493, 497, 488, 484, 498, 494, 485, 489, 480, 490, 486, 481, 482, 320, 320,
]
FIRST = {n: next((code // 4) % 8 for code in STEPS if code // 32 == n) for n in (4, 5, 12, 13)}
WORDS = [
    sum(code << (9 * n) for n, code in enumerate(STEPS[at : at + 3])) for at in range(0, len(STEPS), 3)
]

F32, BF16 = jnp.float32, jnp.bfloat16


def dot(a, b, precision=None):
    return lax.dot_general(
        a, b, (((1,), (0,)), ((), ())), precision=precision, preferred_element_type=F32
    )


def down_rows(row, lanes):
    return jnp.broadcast_to(jnp.broadcast_to(row, (128, 128)).T[:, 0:1], (128, lanes))


def slot_hits(first_id, second_id, expert_of, slot_of):
    rows = first_id.shape[0]
    first, second = first_id == expert_of, second_id == expert_of
    named = jnp.where(first | second, 1.0, 0.0)
    earlier = lax.broadcasted_iota(jnp.int32, (rows, rows), 1) < lax.broadcasted_iota(
        jnp.int32, (rows, rows), 0
    )
    position = dot(jnp.where(earlier, 1.0, 0.0).astype(BF16), named.astype(BF16))
    here = position == slot_of.astype(F32)
    return first, second, jnp.where(here, named, 0.0)


def kernel(
    tok_ref, ids_ref, rw_ref, wg_hbm, wu_hbm, wd_hbm, out_ref,
    wg, wu, wd, xs, part, s_out, s_in, hid, own, pair_out, pair_in,
    c_out, c_in, eo0, eo1, comb, early,
    w_sem, a_ss, a_rs, p_ss, p_rs, x_ss, x_rs, q_ss, q_rs, c_ss, c_rs, y_ss, y_rs,
):
    dp, y, x = lax.axis_index("dp"), lax.axis_index("expert"), lax.axis_index("blk")
    z, c = dp // 2, dp % 2
    width = tok_ref.shape[1]
    sub_w, cut_w = width // SUB, width // CUT
    partner = (z * 2 + (1 - c), y, x)
    right, left, far = (dp, y, (x + 1) % NX), (dp, y, (x + NX - 1) % NX), (dp, y, (x + 2) % NX)
    q_right, q_left, q_far = (x + 1) % NX, (x + NX - 1) % NX, (x + 2) % NX

    def zdev(step):
        return (((z + step + NZ) % NZ) * 2 + c, y, x)

    def ydev(step):
        return (dp, (y + step) % NY, x)

    def zchip(i):
        k = (i + 1) // 2
        return (z + k * (1 - 2 * (i % 2)) + NZ) % NZ

    def remote(src, dst, ss, rs, dev):
        return pltpu.make_async_remote_copy(
            src_ref=src, dst_ref=dst, send_sem=ss, recv_sem=rs, device_id=dev, device_id_type=MESH
        )

    weights = [
        pltpu.make_async_copy(h.at[e], v.at[e], w_sem.at[n, e])
        for e in range(2)
        for n, (h, v) in enumerate(((wg_hbm, wg), (wu_hbm, wu), (wd_hbm, wd)))
    ]
    for w in weights:
        w.start()

    barrier = pltpu.get_barrier_semaphore()
    peers = [partner, zdev(1), zdev(-1), right, left, far, ydev(1), ydev(2), ydev(3)]
    for d in peers:
        pl.semaphore_signal(barrier, inc=1, device_id=d, device_id_type=MESH)

    ids = ids_ref[...].astype(F32)
    id_a, id_b = down_rows(ids[0:1], 128), down_rows(ids[1:2], 128)
    lane = lax.broadcasted_iota(jnp.int32, (128, 128), 1)
    for e in range(2):
        _, _, hit = slot_hits(id_a, id_b, (2 * y + e).astype(F32), lane)
        rows = lax.dot_general(
            hit.astype(BF16), tok_ref[...], (((0,), (0,)), ((), ())), preferred_element_type=F32
        )[:CAP].astype(BF16)
        for s in range(SUB):
            xs[e, s, dp] = rows[:, s * sub_w : (s + 1) * sub_w]
    pl.semaphore_wait(barrier, len(peers))

    def a_copy(e, s, chip, i, up):
        at = xs.at[e, s, 2 * chip + c]
        return remote(at, at, a_ss.at[e, up, s], a_rs.at[e, i, s], zdev(2 * up - 1))

    def p_copy(e, s, chip, i, core):
        at = xs.at[e, s, 2 * chip + core]
        return remote(at, at, p_ss.at[e, s], p_rs.at[e, i, s], partner)

    def send_own(e, s):
        a_copy(e, s, z, 1, 1).start()
        a_copy(e, s, z, 2, 0).start()
        p_copy(e, s, z, 0, c).start()

    def pass_on(e, i, s):
        chip = zchip(i)
        a_copy(e, s, chip, i, 1).wait_recv()

        @pl.when((i < 5) | (i + e == 5) | (i * e == 6))
        def _():
            on = a_copy(e, s, chip, i + 2 - i // 6, i % 2)
            on.wait_send()
            on.start()

        pair = p_copy(e, s, chip, i, c)
        pair.wait_send()
        pair.start()

    def x_copy(v, n):
        d = n % 2
        if n < 2:
            src, dst, way, sem = s_out.at[v, d, 0:2], s_in.at[v, d, 0:2], (right, left)[d], d
        elif n < 4:
            src, dst, way, sem = s_out.at[v, d, 2], s_in.at[v, d, 2], (right, left)[d], 2 + d
        else:
            src, dst, way, sem = hid.at[v, x], hid.at[v, x], (right, left, far)[n - 4], (0, 1, 4)[n - 4]
        return remote(src, dst, x_ss.at[v, (0, 1, 0, 1, 0, 1, 2)[n]], x_rs.at[v, sem], way)

    def x_landed(v, n):
        d = n % 2
        if n < 2:
            at, sem = s_in.at[v, d, 0:2], d
        elif n < 4:
            at, sem = s_in.at[v, d, 2], 2 + d
        else:
            at, sem = hid.at[v, (q_left, q_right, q_far)[n - 4]], (0, 1, 4)[n - 4]
        remote(at, at, x_ss.at[v, 0], x_rs.at[v, sem], right).wait_recv()

    def first(e, i):
        v = e * 8 + i
        chip = zchip(i)

        @pl.when((i == FIRST[4]) & (e == 0))
        def _():
            for n in range(2):
                weights[n].wait()

        @pl.when((i == FIRST[5]) & (e == 1))
        def _():
            for n in range(2):
                weights[3 + n].wait()

        for s in range(SUB):
            p_copy(e, s, chip, i, 1 - c).wait_recv()
        rows = [xs[e, s, pl.ds(2 * chip, 2)].reshape(2 * CAP, sub_w) for s in range(SUB)]
        for g, w in enumerate((wg, wu)):
            total = sum(dot(rows[s], w[e, s * sub_w : (s + 1) * sub_w]) for s in range(SUB))
            for q in range(NX):
                block = total[:, q * 128 : (q + 1) * 128]
                for h in range(2):
                    part[v, q, h, g] = block[h * CAP : (h + 1) * CAP]
        for d, near in enumerate((q_right, q_left)):
            s_out[v, d, 0] = part[v, q_far, d].astype(BF16)
            s_out[v, d, 1] = part[v, near, 1 - d].astype(BF16)
            x_copy(v, d).start()

    def second(e, i):
        v = e * 8 + i
        for d in range(2):
            x_landed(v, d)
        for d, near in enumerate((q_right, q_left)):
            s_out[v, d, 2] = (part[v, near, d] + s_in[v, d, 0].astype(F32)).astype(BF16)
            x_copy(v, d).wait_send()
            x_copy(v, 2 + d).start()

    def third(e, i):
        v = e * 8 + i
        for d in range(2):
            x_landed(v, 2 + d)
        for h in range(2):
            both = part[v, x, h] + s_in[v, h, 2].astype(F32) + s_in[v, 1 - h, 1].astype(F32)
            gate, up = both[0], both[1]
            hid[v, x, h] = (gate / (1.0 + jnp.exp(-gate)) * up).astype(BF16)
        for d in range(2):
            x_copy(v, 2 + d).wait_send()
        for n in range(4, 7):
            x_copy(v, n).start()

    def q_copy(v):
        return remote(pair_out.at[v], pair_in.at[v], q_ss.at[v], q_rs.at[v], partner)

    def sixth(e, i):
        v = e * 8 + i

        @pl.when((i == FIRST[12]) & (e == 0))
        def _():
            weights[2].wait()

        @pl.when((i == FIRST[13]) & (e == 1))
        def _():
            weights[5].wait()

        for n in range(4, 7):
            x_landed(v, n)
        rows = jnp.concatenate(
            [
                jnp.concatenate([hid[v, q, h] for q in range(NX)], axis=1)
                for h in (c, 1 - c)
            ],
            axis=0,
        )
        for n in range(CUT):
            block = dot(rows, wd[e, :, n * cut_w : (n + 1) * cut_w])
            own[v, n] = block[:CAP]
            pair_out[v, n] = block[CAP:]
        q_copy(v).start()
        for n in range(4, 7):
            x_copy(v, n).wait_send()

    def c_copy(e, i, n, up):
        v = e * 8 + i
        return remote(c_out.at[v, n], c_in.at[v, n], c_ss.at[e, up, n], c_rs.at[v, n], zdev(2 * up - 1))

    def y_copy(e, n, o):
        at = (eo0, eo1)[e].at[n, y]
        return remote(at, at, y_ss.at[e, n, o], y_rs.at[e, n, o], ydev(o))

    def y_landed(e, n, o):
        at = (eo0, eo1)[e].at[n, (y + NY - o) % NY]
        remote(at, at, y_ss.at[e, n, o], y_rs.at[e, n, o], ydev(o)).wait_recv()

    def reduce_z(e, i, n):
        v = e * 8 + i
        up = (1 - i % 2) + (i // 7) * e
        no_up = (i == 7) | (i + e == 6)

        @pl.when(n == 0)
        def _():
            q_copy(v).wait_recv()

        def from_up(slot):
            c_copy(e, slot, n, 0).wait_recv()
            return c_in[e * 8 + slot, n].astype(F32)

        @pl.when(no_up)
        def _():
            c_out[v, n] = (own[v, n] + pair_in[v, n]).astype(BF16)

        @pl.when((i > 0) & jnp.logical_not(no_up))
        def _():
            c_out[v, n] = (own[v, n] + pair_in[v, n] + from_up(i + 2 - i // 6)).astype(BF16)
            c_copy(e, i, n, up).wait_send()

        @pl.when(i > 0)
        def _():
            c_copy(e, i, n, up).start()

        @pl.when(i == 0)
        def _():
            total = own[v, n] + pair_in[v, n] + from_up(1) + from_up(2)
            for k in range(2):

                @pl.when(e == k)
                def _():
                    buf = (eo0, eo1)[k]
                    buf[n, y] = total.astype(buf.dtype)
                    for o in range(1, NY):
                        y_copy(k, n, o).start()

    for s in range(SUB):
        send_own(0, s)

    lanes = NY * CAP
    slot = lax.broadcasted_iota(jnp.int32, (128, lanes), 1)
    wide_a, wide_b = down_rows(ids[0:1], lanes), down_rows(ids[1:2], lanes)
    weight_a, weight_b = down_rows(rw_ref[0:1], lanes), down_rows(rw_ref[1:2], lanes)
    for e in range(2):
        expert_of = 2 * (slot // CAP) + e
        one, two, hit = slot_hits(wide_a, wide_b, expert_of.astype(F32), slot % CAP)
        weight = jnp.where(one, weight_a, 0.0) + jnp.where(two, weight_b, 0.0)
        comb[e] = weight * hit

    kinds = (
        pass_on,
        lambda e, i, s: send_own(e, s),
        lambda e, i, s: first(e, i),
        lambda e, i, s: second(e, i),
        lambda e, i, s: third(e, i),
        lambda e, i, s: None,
        lambda e, i, s: sixth(e, i),
        reduce_z,
    )

    def three(t, carry):
        word = jnp.int32(WORDS[-1])
        for n, value in enumerate(WORDS[:-1]):
            word = jnp.where(t == n, jnp.int32(value), word)

        def one(k, word):
            code = word & 511
            kind, e, i, s = code // 64, (code // 32) % 2, (code // 4) % 8, code % 4
            for n, step in enumerate(kinds):
                if n == 5:
                    continue

                @pl.when(kind == n)
                def _():
                    step(e, i, s)

            return word // 512

        lax.fori_loop(0, 3, one, word)
        return carry

    assert len(STEPS) % 3 == 0
    lax.fori_loop(0, len(WORDS), three, 0)

    for n in range(CUT):
        for o in range(1, NY):
            y_landed(0, n, o)
        early[n] = dot(comb[0], eo0[n].reshape(lanes, cut_w), lax.Precision.HIGHEST)

    for e in range(2):

        def sent(i, carry):
            q_copy(e * 8 + i).wait_send()
            return carry

        lax.fori_loop(0, 8, sent, 0)
        for up in range(2):
            for n in range(CUT):
                c_copy(e, 1, n, up).wait_send()
            for s in range(SUB):
                a_copy(e, s, z, 1, up).wait_send()
        for s in range(SUB):
            p_copy(e, s, z, 0, c).wait_send()
    for n in range(CUT):
        for o in range(1, NY):
            y_copy(0, n, o).wait_send()

    high = comb[1].astype(BF16)
    low = (comb[1] - high.astype(F32)).astype(BF16)
    for n in range(CUT):
        for o in range(1, NY):
            y_landed(1, n, o)
        late = eo1[n].reshape(lanes, cut_w)
        out_ref[:, n * cut_w : (n + 1) * cut_w] = (
            early[n] + dot(high, late) + dot(low, late)
        ).astype(BF16)
    for n in range(CUT):
        for o in range(1, NY):
            y_copy(1, n, o).wait_send()


def local(tokens, expert_ids, route_weights, gate_weight, up_weight, down_weight):
    rows, width = tokens.shape
    hidden = gate_weight.shape[2]
    quarter = hidden // NX
    vmem = pl.BlockSpec(memory_space=pltpu.VMEM)
    hbm = pl.BlockSpec(memory_space=pl.ANY)
    dma = pltpu.SemaphoreType.DMA
    return pl.pallas_call(
        kernel,
        out_shape=jax.ShapeDtypeStruct((rows, width), BF16),
        in_specs=[vmem, vmem, vmem, hbm, hbm, hbm],
        out_specs=vmem,
        scratch_shapes=[
            pltpu.VMEM(gate_weight.shape, BF16),
            pltpu.VMEM(up_weight.shape, BF16),
            pltpu.VMEM(down_weight.shape, BF16),
            pltpu.VMEM((2, SUB, 2 * NZ, CAP, width // SUB), BF16),
            pltpu.VMEM((UNITS, NX, 2, 2, CAP, quarter), F32),
            pltpu.VMEM((UNITS, 2, 3, 2, CAP, quarter), BF16),
            pltpu.VMEM((UNITS, 2, 3, 2, CAP, quarter), BF16),
            pltpu.VMEM((UNITS, NX, 2, CAP, quarter), BF16),
            pltpu.VMEM((UNITS, CUT, CAP, width // CUT), F32),
            pltpu.VMEM((UNITS, CUT, CAP, width // CUT), F32),
            pltpu.VMEM((UNITS, CUT, CAP, width // CUT), F32),
            pltpu.VMEM((UNITS, CUT, CAP, width // CUT), BF16),
            pltpu.VMEM((UNITS, CUT, CAP, width // CUT), BF16),
            pltpu.VMEM((CUT, NY, CAP, width // CUT), F32),
            pltpu.VMEM((CUT, NY, CAP, width // CUT), BF16),
            pltpu.VMEM((2, rows, NY * CAP), F32),
            pltpu.VMEM((CUT, rows, width // CUT), F32),
            dma((3, 2)),
            dma((2, 2, SUB)),
            dma((2, 8, SUB)),
            dma((2, SUB)),
            dma((2, 8, SUB)),
            dma((UNITS, 3)),
            dma((UNITS, 5)),
            dma((UNITS,)),
            dma((UNITS,)),
            dma((2, 2, CUT)),
            dma((UNITS, CUT)),
            dma((2, CUT, NY)),
            dma((2, CUT, NY)),
        ],
        compiler_params=pltpu.CompilerParams(
            collective_id=0, has_side_effects=True, vmem_limit_bytes=60 * 2**20
        ),
    )(tokens, expert_ids.T, route_weights.T, gate_weight, up_weight, down_weight)


def solution(mesh):
    placed = (
        P("dp", "blk"),
        P("dp", None),
        P("dp", None),
        P("expert", "blk", "dp"),
        P("expert", "blk", "dp"),
        P("expert", "dp", "blk"),
    )
    return jax.shard_map(
        local, mesh=mesh, in_specs=placed, out_specs=P("dp", "blk"), check_vma=False
    )
```

```python
import functools

import jax
import jax.numpy as jnp
from jax import lax
from jax.experimental import pallas as pl
from jax.experimental.pallas import tpu as pltpu
from jax.sharding import PartitionSpec as P

MESH = pl.DeviceIdType.MESH
CAP = 48
NZ, NY, NX = 8, 4, 4
UNITS = 16
SUB = 2
CUT = 3

STEPS = [
    128, 96, 4, 8, 9, 5, 97, 192, 136, 132, 12, 160, 16, 256, 17, 13,
    40, 200, 144, 140, 196, 41, 20, 168, 21, 25, 36, 24, 264, 208, 152, 28,
    148, 29, 48, 37, 204, 156, 49, 44, 216, 164, 45, 212, 384, 56, 220, 57,
    52, 272, 280, 392, 53, 284, 180, 276, 60, 184, 61, 408, 188, 412, 472, 473,
    244, 268, 476, 477, 478, 172, 404, 400, 252, 260, 474, 468, 176, 464, 465, 469,
    396, 248, 316, 224, 460, 308, 470, 236, 466, 388, 461, 240, 228, 312, 456, 457,
    452, 444, 462, 232, 508, 458, 436, 453, 300, 448, 304, 509, 500, 501, 440, 510,
    502, 292, 504, 449, 454, 296, 428, 432, 505, 492, 288, 496, 493, 494, 420, 506,
    424, 450, 497, 484, 488, 485, 498, 416, 486, 489, 480, 490, 481, 482, 320, 320,
]
FIRST = {n: next((code // 4) % 8 for code in STEPS if code // 32 == n) for n in (4, 5, 12, 13)}
WORDS = [
    sum(code << (9 * n) for n, code in enumerate(STEPS[at : at + 3])) for at in range(0, len(STEPS), 3)
]

F32, BF16 = jnp.float32, jnp.bfloat16


def dot(a, b, precision=None):
    return lax.dot_general(
        a, b, (((1,), (0,)), ((), ())), precision=precision, preferred_element_type=F32
    )


def down_rows(row, lanes):
    return jnp.broadcast_to(jnp.broadcast_to(row, (128, 128)).T[:, 0:1], (128, lanes))


def slot_hits(first_id, second_id, expert_of, slot_of):
    rows = first_id.shape[0]
    first, second = first_id == expert_of, second_id == expert_of
    named = jnp.where(first | second, 1.0, 0.0)
    earlier = lax.broadcasted_iota(jnp.int32, (rows, rows), 1) < lax.broadcasted_iota(
        jnp.int32, (rows, rows), 0
    )
    position = dot(jnp.where(earlier, 1.0, 0.0).astype(BF16), named.astype(BF16))
    here = position == slot_of.astype(F32)
    return first, second, jnp.where(here, named, 0.0)


def kernel(
    tok_ref, ids_ref, rw_ref, wg_hbm, wu_hbm, wd_hbm, out_ref,
    wg, wu, wd, xs, part, s_out, s_in, hid, own, pair_out, pair_in,
    c_out, c_in, eo0, eo1, comb, early,
    w_sem, a_ss, a_rs, p_ss, p_rs, x_ss, x_rs, q_ss, q_rs, c_ss, c_rs, y_ss, y_rs,
):
    dp, y, x = lax.axis_index("dp"), lax.axis_index("expert"), lax.axis_index("blk")
    z, c = dp // 2, dp % 2
    width = tok_ref.shape[1]
    sub_w, cut_w = width // SUB, width // CUT
    partner = (z * 2 + (1 - c), y, x)
    right, left, far = (dp, y, (x + 1) % NX), (dp, y, (x + NX - 1) % NX), (dp, y, (x + 2) % NX)
    q_right, q_left, q_far = (x + 1) % NX, (x + NX - 1) % NX, (x + 2) % NX

    def zdev(step):
        return (((z + step + NZ) % NZ) * 2 + c, y, x)

    def ydev(step):
        return (dp, (y + step) % NY, x)

    def zchip(i):
        k = (i + 1) // 2
        return (z + k * (1 - 2 * (i % 2)) + NZ) % NZ

    def remote(src, dst, ss, rs, dev):
        return pltpu.make_async_remote_copy(
            src_ref=src, dst_ref=dst, send_sem=ss, recv_sem=rs, device_id=dev, device_id_type=MESH
        )

    weights = [
        pltpu.make_async_copy(h.at[e], v.at[e], w_sem.at[n, e])
        for e in range(2)
        for n, (h, v) in enumerate(((wg_hbm, wg), (wu_hbm, wu), (wd_hbm, wd)))
    ]
    for w in weights:
        w.start()

    barrier = pltpu.get_barrier_semaphore()
    peers = [partner, zdev(1), zdev(-1), right, left, far, ydev(1), ydev(2), ydev(3)]
    for d in peers:
        pl.semaphore_signal(barrier, inc=1, device_id=d, device_id_type=MESH)

    ids = ids_ref[...].astype(F32)
    id_a, id_b = down_rows(ids[0:1], 128), down_rows(ids[1:2], 128)
    lane = lax.broadcasted_iota(jnp.int32, (128, 128), 1)
    for e in range(2):
        _, _, hit = slot_hits(id_a, id_b, (2 * y + e).astype(F32), lane)
        rows = lax.dot_general(
            hit.astype(BF16), tok_ref[...], (((0,), (0,)), ((), ())), preferred_element_type=F32
        )[:CAP].astype(BF16)
        for s in range(SUB):
            xs[e, s, dp] = rows[:, s * sub_w : (s + 1) * sub_w]
    pl.semaphore_wait(barrier, len(peers))

    def a_copy(e, s, chip, i, up):
        at = xs.at[e, s, 2 * chip + c]
        return remote(at, at, a_ss.at[e, up, s], a_rs.at[e, i, s], zdev(2 * up - 1))

    def p_copy(e, s, chip, i, core):
        at = xs.at[e, s, 2 * chip + core]
        return remote(at, at, p_ss.at[e, s], p_rs.at[e, i], partner)

    def send_own(e, s):
        a_copy(e, s, z, 1, 1).start()
        a_copy(e, s, z, 2, 0).start()
        p_copy(e, s, z, 0, c).start()

    def pass_on(e, i, s):
        chip = zchip(i)
        a_copy(e, s, chip, i, 1).wait_recv()

        @pl.when((i < 5) | (i + e == 5) | (i * e == 6))
        def _():
            on = a_copy(e, s, chip, i + 2 - i // 6, i % 2)
            on.wait_send()
            on.start()

        pair = p_copy(e, s, chip, i, c)
        pair.wait_send()
        pair.start()

    def x_copy(v, n):
        d = n % 2
        if n < 2:
            at, way, stage = (s_out.at[v, d, 0:2], s_in.at[v, d, 0:2]), (right, left)[d], 0
        elif n < 4:
            at, way, stage = (s_out.at[v, d, 2], s_in.at[v, d, 2]), (right, left)[d], 1
        else:
            at, way, stage = (hid.at[v, x], hid.at[v, x]), (right, left, far)[n - 4], 2
        return remote(*at, x_ss.at[v], x_rs.at[v, stage], way)

    def x_all(v, stage):
        at = (s_in.at[v, :, 0:2], s_in.at[v, :, 2], hid.at[v, 0:3])[stage]
        return remote(at, at, x_ss.at[v], x_rs.at[v, stage], right)

    def first(e, i):
        v = e * 8 + i
        chip = zchip(i)

        @pl.when((i == FIRST[4]) & (e == 0))
        def _():
            for n in range(2):
                weights[n].wait()

        @pl.when((i == FIRST[5]) & (e == 1))
        def _():
            for n in range(2):
                weights[3 + n].wait()

        at = xs.at[e, :, 2 * chip + 1 - c]
        remote(at, at, p_ss.at[e, 0], p_rs.at[e, i], partner).wait_recv()
        rows = [xs[e, s, pl.ds(2 * chip, 2)].reshape(2 * CAP, sub_w) for s in range(SUB)]
        for g, w in enumerate((wg, wu)):
            total = sum(dot(rows[s], w[e, s * sub_w : (s + 1) * sub_w]) for s in range(SUB))
            for q in range(NX):
                block = total[:, q * 128 : (q + 1) * 128]
                for h in range(2):
                    part[v, q, h, g] = block[h * CAP : (h + 1) * CAP]
        for d, near in enumerate((q_right, q_left)):
            s_out[v, d, 0] = part[v, q_far, d].astype(BF16)
            s_out[v, d, 1] = part[v, near, 1 - d].astype(BF16)
            x_copy(v, d).start()

    def second(e, i):
        v = e * 8 + i
        x_all(v, 0).wait()
        for d, near in enumerate((q_right, q_left)):
            s_out[v, d, 2] = (part[v, near, d] + s_in[v, d, 0].astype(F32)).astype(BF16)
            x_copy(v, 2 + d).start()

    def third(e, i):
        v = e * 8 + i
        x_all(v, 1).wait()
        for h in range(2):
            both = part[v, x, h] + s_in[v, h, 2].astype(F32) + s_in[v, 1 - h, 1].astype(F32)
            gate, up = both[0], both[1]
            hid[v, x, h] = (gate / (1.0 + jnp.exp(-gate)) * up).astype(BF16)
        for n in range(4, 7):
            x_copy(v, n).start()

    def q_copy(v):
        return remote(pair_out.at[v], pair_in.at[v], q_ss.at[0], q_rs.at[v], partner)

    def sixth(e, i):
        v = e * 8 + i

        @pl.when((i == FIRST[12]) & (e == 0))
        def _():
            weights[2].wait()

        @pl.when((i == FIRST[13]) & (e == 1))
        def _():
            weights[5].wait()

        x_all(v, 2).wait()
        rows = jnp.concatenate(
            [
                jnp.concatenate([hid[v, q, h] for q in range(NX)], axis=1)
                for h in (c, 1 - c)
            ],
            axis=0,
        )
        for n in range(CUT):
            block = dot(rows, wd[e, :, n * cut_w : (n + 1) * cut_w])
            own[v, n] = block[:CAP]
            pair_out[v, n] = block[CAP:]
        q_copy(v).start()

    def c_copy(e, i, n, up):
        v = e * 8 + i
        return remote(c_out.at[v, n], c_in.at[v, n], c_ss.at[e, up, n], c_rs.at[v, n], zdev(2 * up - 1))

    def y_copy(e, n, o):
        at = (eo0, eo1)[e].at[n, y]
        return remote(at, at, y_ss.at[e], y_rs.at[e, n], ydev(o))

    def y_all(e, n):
        at = (eo0, eo1)[e].at[n, 1:NY]
        return remote(at, at, y_ss.at[e], y_rs.at[e, n], ydev(1))

    def y_sent(e):
        at = (eo0, eo1)[e].at[:, 1:NY]
        remote(at, at, y_ss.at[e], y_rs.at[e, 0], ydev(1)).wait_send()

    def reduce_z(e, i, n):
        v = e * 8 + i
        up = (1 - i % 2) + (i // 7) * e
        no_up = (i == 7) | (i + e == 6)

        @pl.when(n == 0)
        def _():
            q_copy(v).wait_recv()

        def from_up(slot):
            c_copy(e, slot, n, 0).wait_recv()
            return c_in[e * 8 + slot, n].astype(F32)

        @pl.when(no_up)
        def _():
            c_out[v, n] = (own[v, n] + pair_in[v, n]).astype(BF16)

        @pl.when((i > 0) & jnp.logical_not(no_up))
        def _():
            c_out[v, n] = (own[v, n] + pair_in[v, n] + from_up(i + 2 - i // 6)).astype(BF16)
            c_copy(e, i, n, up).wait_send()

        @pl.when(i > 0)
        def _():
            c_copy(e, i, n, up).start()

        @pl.when(i == 0)
        def _():
            total = own[v, n] + pair_in[v, n] + from_up(1) + from_up(2)
            for k in range(2):

                @pl.when(e == k)
                def _():
                    buf = (eo0, eo1)[k]
                    buf[n, y] = total.astype(buf.dtype)
                    for o in range(1, NY):
                        y_copy(k, n, o).start()

    for s in range(SUB):
        send_own(0, s)

    kinds = (
        pass_on,
        lambda e, i, s: send_own(e, s),
        lambda e, i, s: first(e, i),
        lambda e, i, s: second(e, i),
        lambda e, i, s: third(e, i),
        lambda e, i, s: None,
        lambda e, i, s: sixth(e, i),
        reduce_z,
    )

    def three(t, carry):
        word = jnp.int32(WORDS[-1])
        for n, value in enumerate(WORDS[:-1]):
            word = jnp.where(t == n, jnp.int32(value), word)

        def one(k, word):
            code = word & 511
            kind, e, i, s = code // 64, (code // 32) % 2, (code // 4) % 8, code % 4
            for n, step in enumerate(kinds):
                if n == 5:
                    continue

                @pl.when(kind == n)
                def _():
                    step(e, i, s)

            return word // 512

        lax.fori_loop(0, 3, one, word)
        return carry

    assert len(STEPS) % 3 == 0
    lax.fori_loop(0, len(WORDS), three, 0)

    lanes = NY * CAP
    slot = lax.broadcasted_iota(jnp.int32, (128, lanes), 1)
    wide_a, wide_b = down_rows(ids[0:1], lanes), down_rows(ids[1:2], lanes)
    weight_a, weight_b = down_rows(rw_ref[0:1], lanes), down_rows(rw_ref[1:2], lanes)
    for e in range(2):
        expert_of = 2 * (slot // CAP) + e
        one, two, hit = slot_hits(wide_a, wide_b, expert_of.astype(F32), slot % CAP)
        weight = jnp.where(one, weight_a, 0.0) + jnp.where(two, weight_b, 0.0)
        comb[e] = weight * hit

    for n in range(CUT):
        y_all(0, n).wait_recv()
        early[n] = dot(comb[0], eo0[n].reshape(lanes, cut_w), lax.Precision.HIGHEST)

    remote(pair_out, pair_in, q_ss.at[0], q_rs.at[0], partner).wait_send()
    for e in range(2):

        for up in range(2):
            for n in range(CUT):
                c_copy(e, 1, n, up).wait_send()
            for s in range(SUB):
                a_copy(e, s, z, 1, up).wait_send()
        for s in range(SUB):
            p_copy(e, s, z, 0, c).wait_send()
    y_sent(0)

    high = comb[1].astype(BF16)
    low = (comb[1] - high.astype(F32)).astype(BF16)
    for n in range(CUT):
        y_all(1, n).wait_recv()
        late = eo1[n].reshape(lanes, cut_w)
        out_ref[:, n * cut_w : (n + 1) * cut_w] = (
            early[n] + dot(high, late) + dot(low, late)
        ).astype(BF16)
    y_sent(1)


def local(tokens, expert_ids, route_weights, gate_weight, up_weight, down_weight):
    rows, width = tokens.shape
    hidden = gate_weight.shape[2]
    quarter = hidden // NX
    vmem = pl.BlockSpec(memory_space=pltpu.VMEM)
    hbm = pl.BlockSpec(memory_space=pl.ANY)
    dma = pltpu.SemaphoreType.DMA
    return pl.pallas_call(
        kernel,
        out_shape=jax.ShapeDtypeStruct((rows, width), BF16),
        in_specs=[vmem, vmem, vmem, hbm, hbm, hbm],
        out_specs=vmem,
        scratch_shapes=[
            pltpu.VMEM(gate_weight.shape, BF16),
            pltpu.VMEM(up_weight.shape, BF16),
            pltpu.VMEM(down_weight.shape, BF16),
            pltpu.VMEM((2, SUB, 2 * NZ, CAP, width // SUB), BF16),
            pltpu.VMEM((UNITS, NX, 2, 2, CAP, quarter), F32),
            pltpu.VMEM((UNITS, 2, 3, 2, CAP, quarter), BF16),
            pltpu.VMEM((UNITS, 2, 3, 2, CAP, quarter), BF16),
            pltpu.VMEM((UNITS, NX, 2, CAP, quarter), BF16),
            pltpu.VMEM((UNITS, CUT, CAP, width // CUT), F32),
            pltpu.VMEM((UNITS, CUT, CAP, width // CUT), F32),
            pltpu.VMEM((UNITS, CUT, CAP, width // CUT), F32),
            pltpu.VMEM((UNITS, CUT, CAP, width // CUT), BF16),
            pltpu.VMEM((UNITS, CUT, CAP, width // CUT), BF16),
            pltpu.VMEM((CUT, NY, CAP, width // CUT), F32),
            pltpu.VMEM((CUT, NY, CAP, width // CUT), BF16),
            pltpu.VMEM((2, rows, NY * CAP), F32),
            pltpu.VMEM((CUT, rows, width // CUT), F32),
            dma((3, 2)),
            dma((2, 2, SUB)),
            dma((2, 8, SUB)),
            dma((2, SUB)),
            dma((2, 8)),
            dma((UNITS,)),
            dma((UNITS, 3)),
            dma((1,)),
            dma((UNITS,)),
            dma((2, 2, CUT)),
            dma((UNITS, CUT)),
            dma((2,)),
            dma((2, CUT)),
        ],
        compiler_params=pltpu.CompilerParams(
            collective_id=0, has_side_effects=True, vmem_limit_bytes=60 * 2**20
        ),
    )(tokens, expert_ids.T, route_weights.T, gate_weight, up_weight, down_weight)


def solution(mesh):
    placed = (
        P("dp", "blk"),
        P("dp", None),
        P("dp", None),
        P("expert", "blk", "dp"),
        P("expert", "blk", "dp"),
        P("expert", "dp", "blk"),
    )
    return jax.shard_map(
        local, mesh=mesh, in_specs=placed, out_specs=P("dp", "blk"), check_vma=False
    )
```

```python
import functools

import jax
import jax.numpy as jnp
from jax import lax
from jax.experimental import pallas as pl
from jax.experimental.pallas import tpu as pltpu
from jax.sharding import PartitionSpec as P

MESH = pl.DeviceIdType.MESH
CAP = 48
NZ, NY, NX = 8, 4, 4
UNITS = 16
SUB = 2
CUT = 3

STEPS = [
    128, 96, 4, 8, 9, 5, 97, 192, 136, 132, 12, 160, 16, 256, 17, 13,
    40, 200, 144, 140, 196, 41, 20, 168, 21, 25, 36, 24, 264, 208, 152, 28,
    148, 29, 48, 37, 204, 156, 49, 44, 216, 164, 45, 212, 384, 56, 220, 57,
    52, 272, 280, 392, 53, 284, 180, 276, 60, 184, 61, 408, 188, 412, 472, 473,
    244, 268, 476, 477, 478, 172, 404, 400, 252, 260, 474, 468, 176, 464, 465, 469,
    396, 248, 316, 224, 460, 308, 470, 236, 466, 388, 461, 240, 228, 312, 456, 457,
    452, 444, 462, 232, 508, 458, 436, 453, 300, 448, 304, 509, 500, 501, 440, 510,
    502, 292, 504, 449, 454, 296, 428, 432, 505, 492, 288, 496, 493, 494, 420, 506,
    424, 450, 497, 484, 488, 485, 498, 416, 486, 489, 480, 490, 481, 482, 320, 320,
]
FIRST = {n: next((code // 4) % 8 for code in STEPS if code // 32 == n) for n in (4, 5, 12, 13)}
WORDS = [
    sum(code << (9 * n) for n, code in enumerate(STEPS[at : at + 3])) for at in range(0, len(STEPS), 3)
]

F32, BF16 = jnp.float32, jnp.bfloat16


def dot(a, b, precision=None):
    return lax.dot_general(
        a, b, (((1,), (0,)), ((), ())), precision=precision, preferred_element_type=F32
    )


def down_rows(row, lanes):
    return jnp.broadcast_to(jnp.broadcast_to(row, (128, 128)).T[:, 0:1], (128, lanes))


def slot_hits(first_id, second_id, expert_of, slot_of):
    rows = first_id.shape[0]
    first, second = first_id == expert_of, second_id == expert_of
    named = jnp.where(first | second, 1.0, 0.0)
    earlier = lax.broadcasted_iota(jnp.int32, (rows, rows), 1) < lax.broadcasted_iota(
        jnp.int32, (rows, rows), 0
    )
    position = dot(jnp.where(earlier, 1.0, 0.0).astype(BF16), named.astype(BF16))
    here = position == slot_of.astype(F32)
    return first, second, jnp.where(here, named, 0.0)


def kernel(
    tok_ref, ids_ref, rw_ref, wg_hbm, wu_hbm, wd_hbm, out_ref,
    wg, wu, wd, xs, part, s_out, s_in, hid, own, pair_out, pair_in,
    c_out, c_in, eo0, eo1, comb, early,
    w_sem, a_ss, a_rs, p_ss, p_rs, x_ss, x_rs, q_ss, q_rs, c_ss, c_rs, y_ss, y_rs,
):
    dp, y, x = lax.axis_index("dp"), lax.axis_index("expert"), lax.axis_index("blk")
    z, c = dp // 2, dp % 2
    width = tok_ref.shape[1]
    sub_w, cut_w = width // SUB, width // CUT
    partner = (z * 2 + (1 - c), y, x)
    right, left, far = (dp, y, (x + 1) % NX), (dp, y, (x + NX - 1) % NX), (dp, y, (x + 2) % NX)
    q_right, q_left, q_far = (x + 1) % NX, (x + NX - 1) % NX, (x + 2) % NX

    def zdev(step):
        return (((z + step + NZ) % NZ) * 2 + c, y, x)

    def ydev(step):
        return (dp, (y + step) % NY, x)

    def zchip(i):
        k = (i + 1) // 2
        return (z + k * (1 - 2 * (i % 2)) + NZ) % NZ

    def remote(src, dst, ss, rs, dev):
        return pltpu.make_async_remote_copy(
            src_ref=src, dst_ref=dst, send_sem=ss, recv_sem=rs, device_id=dev, device_id_type=MESH
        )

    weights = [
        pltpu.make_async_copy(h.at[e], v.at[e], w_sem.at[n, e])
        for e in range(2)
        for n, (h, v) in enumerate(((wg_hbm, wg), (wu_hbm, wu), (wd_hbm, wd)))
    ]

    barrier = pltpu.get_barrier_semaphore()
    peers = [partner, zdev(1), zdev(-1), right, left, far, ydev(1), ydev(2), ydev(3)]
    for d in peers:
        pl.semaphore_signal(barrier, inc=1, device_id=d, device_id_type=MESH)
    for w in weights:
        w.start()

    ids = ids_ref[...].astype(F32)
    id_a, id_b = down_rows(ids[0:1], 128), down_rows(ids[1:2], 128)
    lane = lax.broadcasted_iota(jnp.int32, (128, 128), 1)
    def pick(e):
        _, _, hit = slot_hits(id_a, id_b, (2 * y + e).astype(F32), lane)
        rows = lax.dot_general(
            hit.astype(BF16), tok_ref[...], (((0,), (0,)), ((), ())), preferred_element_type=F32
        )[:CAP].astype(BF16)
        for s in range(SUB):
            xs[e, s, dp] = rows[:, s * sub_w : (s + 1) * sub_w]
    pick(0)
    pl.semaphore_wait(barrier, len(peers))

    def a_copy(e, s, chip, i, up):
        at = xs.at[e, s, 2 * chip + c]
        return remote(at, at, a_ss.at[e, up, s], a_rs.at[e, i, s], zdev(2 * up - 1))

    def p_copy(e, s, chip, i, core):
        at = xs.at[e, s, 2 * chip + core]
        return remote(at, at, p_ss.at[e, s], p_rs.at[e, i], partner)

    def send_own(e, s):
        a_copy(e, s, z, 1, 1).start()
        a_copy(e, s, z, 2, 0).start()
        p_copy(e, s, z, 0, c).start()

    def pass_on(e, i, s):
        chip = zchip(i)
        a_copy(e, s, chip, i, 1).wait_recv()

        @pl.when((i < 5) | (i + e == 5) | (i * e == 6))
        def _():
            on = a_copy(e, s, chip, i + 2 - i // 6, i % 2)
            on.wait_send()
            on.start()

        pair = p_copy(e, s, chip, i, c)
        pair.wait_send()
        pair.start()

    def x_copy(v, n):
        d = n % 2
        if n < 2:
            at, way, stage = (s_out.at[v, d, 0:2], s_in.at[v, d, 0:2]), (right, left)[d], 0
        elif n < 4:
            at, way, stage = (s_out.at[v, d, 2], s_in.at[v, d, 2]), (right, left)[d], 1
        else:
            at, way, stage = (hid.at[v, x], hid.at[v, x]), (right, left, far)[n - 4], 2
        return remote(*at, x_ss.at[v], x_rs.at[v, stage], way)

    def x_all(v, stage):
        at = (s_in.at[v, :, 0:2], s_in.at[v, :, 2], hid.at[v, 0:3])[stage]
        return remote(at, at, x_ss.at[v], x_rs.at[v, stage], right)

    def first(e, i):
        v = e * 8 + i
        chip = zchip(i)

        @pl.when((i == FIRST[4]) & (e == 0))
        def _():
            for n in range(2):
                weights[n].wait()

        @pl.when((i == FIRST[5]) & (e == 1))
        def _():
            for n in range(2):
                weights[3 + n].wait()

        at = xs.at[e, :, 2 * chip + 1 - c]
        remote(at, at, p_ss.at[e, 0], p_rs.at[e, i], partner).wait_recv()
        rows = [xs[e, s, pl.ds(2 * chip, 2)].reshape(2 * CAP, sub_w) for s in range(SUB)]
        for g, w in enumerate((wg, wu)):
            total = sum(dot(rows[s], w[e, s * sub_w : (s + 1) * sub_w]) for s in range(SUB))
            for q in range(NX):
                block = total[:, q * 128 : (q + 1) * 128]
                for h in range(2):
                    part[v, q, h, g] = block[h * CAP : (h + 1) * CAP]
        for d, near in enumerate((q_right, q_left)):
            s_out[v, d, 0] = part[v, q_far, d].astype(BF16)
            s_out[v, d, 1] = part[v, near, 1 - d].astype(BF16)
            x_copy(v, d).start()

    def second(e, i):
        v = e * 8 + i
        x_all(v, 0).wait()
        for d, near in enumerate((q_right, q_left)):
            s_out[v, d, 2] = (part[v, near, d] + s_in[v, d, 0].astype(F32)).astype(BF16)
            x_copy(v, 2 + d).start()

    def third(e, i):
        v = e * 8 + i
        x_all(v, 1).wait()
        for h in range(2):
            both = part[v, x, h] + s_in[v, h, 2].astype(F32) + s_in[v, 1 - h, 1].astype(F32)
            gate, up = both[0], both[1]
            hid[v, x, h] = (gate / (1.0 + jnp.exp(-gate)) * up).astype(BF16)
        for n in range(4, 7):
            x_copy(v, n).start()

    def q_copy(v):
        return remote(pair_out.at[v], pair_in.at[v], q_ss.at[0], q_rs.at[v], partner)

    def sixth(e, i):
        v = e * 8 + i

        @pl.when((i == FIRST[12]) & (e == 0))
        def _():
            weights[2].wait()

        @pl.when((i == FIRST[13]) & (e == 1))
        def _():
            weights[5].wait()

        x_all(v, 2).wait()
        rows = jnp.concatenate(
            [
                jnp.concatenate([hid[v, q, h] for q in range(NX)], axis=1)
                for h in (c, 1 - c)
            ],
            axis=0,
        )
        for n in range(CUT):
            block = dot(rows, wd[e, :, n * cut_w : (n + 1) * cut_w])
            own[v, n] = block[:CAP]
            pair_out[v, n] = block[CAP:]
        q_copy(v).start()

    def c_copy(e, i, n, up):
        v = e * 8 + i
        return remote(c_out.at[v, n], c_in.at[v, n], c_ss.at[e, up, n], c_rs.at[v, n], zdev(2 * up - 1))

    def y_copy(e, n, o):
        at = (eo0, eo1)[e].at[n, y]
        return remote(at, at, y_ss.at[e], y_rs.at[e, n], ydev(o))

    def y_all(e, n):
        at = (eo0, eo1)[e].at[n, 1:NY]
        return remote(at, at, y_ss.at[e], y_rs.at[e, n], ydev(1))

    def y_sent(e):
        at = (eo0, eo1)[e].at[:, 1:NY]
        remote(at, at, y_ss.at[e], y_rs.at[e, 0], ydev(1)).wait_send()

    def reduce_z(e, i, n):
        v = e * 8 + i
        up = (1 - i % 2) + (i // 7) * e
        no_up = (i == 7) | (i + e == 6)

        @pl.when(n == 0)
        def _():
            q_copy(v).wait_recv()

        def from_up(slot):
            c_copy(e, slot, n, 0).wait_recv()
            return c_in[e * 8 + slot, n].astype(F32)

        @pl.when(no_up)
        def _():
            c_out[v, n] = (own[v, n] + pair_in[v, n]).astype(BF16)

        @pl.when((i > 0) & jnp.logical_not(no_up))
        def _():
            c_out[v, n] = (own[v, n] + pair_in[v, n] + from_up(i + 2 - i // 6)).astype(BF16)
            c_copy(e, i, n, up).wait_send()

        @pl.when(i > 0)
        def _():
            c_copy(e, i, n, up).start()

        @pl.when(i == 0)
        def _():
            total = own[v, n] + pair_in[v, n] + from_up(1) + from_up(2)
            for k in range(2):

                @pl.when(e == k)
                def _():
                    buf = (eo0, eo1)[k]
                    buf[n, y] = total.astype(buf.dtype)
                    for o in range(1, NY):
                        y_copy(k, n, o).start()

    for s in range(SUB):
        send_own(0, s)
    pick(1)

    kinds = (
        pass_on,
        lambda e, i, s: send_own(e, s),
        lambda e, i, s: first(e, i),
        lambda e, i, s: second(e, i),
        lambda e, i, s: third(e, i),
        lambda e, i, s: None,
        lambda e, i, s: sixth(e, i),
        reduce_z,
    )

    def three(t, carry):
        word = jnp.int32(WORDS[-1])
        for n, value in enumerate(WORDS[:-1]):
            word = jnp.where(t == n, jnp.int32(value), word)

        def one(k, word):
            code = word & 511
            kind, e, i, s = code // 64, (code // 32) % 2, (code // 4) % 8, code % 4
            for n, step in enumerate(kinds):
                if n == 5:
                    continue

                @pl.when(kind == n)
                def _():
                    step(e, i, s)

            return word // 512

        lax.fori_loop(0, 3, one, word)
        return carry

    assert len(STEPS) % 3 == 0
    lax.fori_loop(0, len(WORDS), three, 0)

    lanes = NY * CAP
    slot = lax.broadcasted_iota(jnp.int32, (128, lanes), 1)
    wide_a, wide_b = down_rows(ids[0:1], lanes), down_rows(ids[1:2], lanes)
    weight_a, weight_b = down_rows(rw_ref[0:1], lanes), down_rows(rw_ref[1:2], lanes)
    for e in range(2):
        expert_of = 2 * (slot // CAP) + e
        one, two, hit = slot_hits(wide_a, wide_b, expert_of.astype(F32), slot % CAP)
        weight = jnp.where(one, weight_a, 0.0) + jnp.where(two, weight_b, 0.0)
        comb[e] = weight * hit

    for n in range(CUT):
        y_all(0, n).wait_recv()
        early[n] = dot(comb[0], eo0[n].reshape(lanes, cut_w), lax.Precision.HIGHEST)

    remote(pair_out, pair_in, q_ss.at[0], q_rs.at[0], partner).wait_send()
    for e in range(2):

        for up in range(2):
            for n in range(CUT):
                c_copy(e, 1, n, up).wait_send()
            for s in range(SUB):
                a_copy(e, s, z, 1, up).wait_send()
        for s in range(SUB):
            p_copy(e, s, z, 0, c).wait_send()
    y_sent(0)

    high = comb[1].astype(BF16)
    low = (comb[1] - high.astype(F32)).astype(BF16)
    for n in range(CUT):
        y_all(1, n).wait_recv()
        late = eo1[n].reshape(lanes, cut_w)
        out_ref[:, n * cut_w : (n + 1) * cut_w] = (
            early[n] + dot(high, late) + dot(low, late)
        ).astype(BF16)
    y_sent(1)


def local(tokens, expert_ids, route_weights, gate_weight, up_weight, down_weight):
    rows, width = tokens.shape
    hidden = gate_weight.shape[2]
    quarter = hidden // NX
    vmem = pl.BlockSpec(memory_space=pltpu.VMEM)
    hbm = pl.BlockSpec(memory_space=pl.ANY)
    dma = pltpu.SemaphoreType.DMA
    return pl.pallas_call(
        kernel,
        out_shape=jax.ShapeDtypeStruct((rows, width), BF16),
        in_specs=[vmem, vmem, vmem, hbm, hbm, hbm],
        out_specs=vmem,
        scratch_shapes=[
            pltpu.VMEM(gate_weight.shape, BF16),
            pltpu.VMEM(up_weight.shape, BF16),
            pltpu.VMEM(down_weight.shape, BF16),
            pltpu.VMEM((2, SUB, 2 * NZ, CAP, width // SUB), BF16),
            pltpu.VMEM((UNITS, NX, 2, 2, CAP, quarter), F32),
            pltpu.VMEM((UNITS, 2, 3, 2, CAP, quarter), BF16),
            pltpu.VMEM((UNITS, 2, 3, 2, CAP, quarter), BF16),
            pltpu.VMEM((UNITS, NX, 2, CAP, quarter), BF16),
            pltpu.VMEM((UNITS, CUT, CAP, width // CUT), F32),
            pltpu.VMEM((UNITS, CUT, CAP, width // CUT), F32),
            pltpu.VMEM((UNITS, CUT, CAP, width // CUT), F32),
            pltpu.VMEM((UNITS, CUT, CAP, width // CUT), BF16),
            pltpu.VMEM((UNITS, CUT, CAP, width // CUT), BF16),
            pltpu.VMEM((CUT, NY, CAP, width // CUT), F32),
            pltpu.VMEM((CUT, NY, CAP, width // CUT), BF16),
            pltpu.VMEM((2, rows, NY * CAP), F32),
            pltpu.VMEM((CUT, rows, width // CUT), F32),
            dma((3, 2)),
            dma((2, 2, SUB)),
            dma((2, 8, SUB)),
            dma((2, SUB)),
            dma((2, 8)),
            dma((UNITS,)),
            dma((UNITS, 3)),
            dma((1,)),
            dma((UNITS,)),
            dma((2, 2, CUT)),
            dma((UNITS, CUT)),
            dma((2,)),
            dma((2, CUT)),
        ],
        compiler_params=pltpu.CompilerParams(
            collective_id=0, has_side_effects=True, vmem_limit_bytes=60 * 2**20
        ),
    )(tokens, expert_ids.T, route_weights.T, gate_weight, up_weight, down_weight)


def solution(mesh):
    placed = (
        P("dp", "blk"),
        P("dp", None),
        P("dp", None),
        P("expert", "blk", "dp"),
        P("expert", "blk", "dp"),
        P("expert", "dp", "blk"),
    )
    return jax.shard_map(
        local, mesh=mesh, in_specs=placed, out_specs=P("dp", "blk"), check_vma=False
    )
```
